512 devices in a mesh: dp: 64 (over x_lo, z, core), cuts: 8 (over y, x_hi).
Axes of the slice: x: 4 (x_hi: 2, x_lo: 2; x = x_hi * 2 + x_lo), y: 4, z: 16, core: 2. Of those that a mesh axis runs over, the one named last changes fastest.
Arguments:
- prompt_features: bfloat16 [16384, 1024], P('dp'), may hold values from -64 to 64
- refusal_features: bfloat16 [16384, 1024], P('dp'), may hold values from -64 to 64
- projection: bfloat16 [1024, 1024], P(None, 'cuts'), may hold values from -0.1875 to 0.1875
- positives: int32 [16384], P('dp'), may hold values from 0 to 255, as said below
Outputs:
- projection_grad: float32 [1024, 1024], P(None, 'cuts')
The draws below stay inside these ranges and needn't reach their ends.
Inputs may be any that keep to these rules, and one draw needn't show every extreme that they name: `positives`: within each aligned block of 256 prompts, a permutation of 0 to 255.
All inputs are finite; a program needn't handle non-finite values.
Results may differ from the reference program's by a relative error of at most 0.0021.
The reference program's roundings to bfloat16 on the way count: a program that leaves them out, or rounds other values in their place, can miss the bound.
Values may be sent and summed in bfloat16 or wider, within the bound.
No kernel may reach another device: no remote copies, remote signals or barrier semaphores. Data moves between devices by JAX's collectives and lax.ppermute only.
A program may use at most 64 MiB of HBM per device.

```python
import jax
import jax.numpy as jnp
from jax import lax

D = 1024
E = 1024
ROWS = 256
N = 16384
N_DP = 64


def rising(fraction, ratio):
    return jnp.exp(jnp.log(ratio) * (fraction - 0.5))[:, None]


def shard_fraction():
    shard = (jnp.arange(N, dtype=jnp.int32) // ROWS).astype(jnp.float32)
    return shard / max(N // ROWS - 1, 1)


def inner_fraction():
    inner = (jnp.arange(N, dtype=jnp.int32) % ROWS).astype(jnp.float32)
    return inner / max(ROWS - 1, 1)


def draw_refusal_features(key, part):
    table = jnp.clip(jax.random.normal(key, (N, D), jnp.float32), -6.0, 6.0) * rising(inner_fraction(), 4.0)
    return table.astype(jnp.bfloat16)


def draw_prompt_features(key, part):
    own = jax.random.fold_in(key, 11)
    values = jnp.clip(jax.random.normal(own, (N, D), jnp.float32), -6.0, 6.0) * rising(shard_fraction(), 4.0)
    return values.astype(jnp.bfloat16)


def draw_positives(key, part):
    key = jax.random.fold_in(key, 5)
    block_keys = jax.random.split(key, N // ROWS)
    orders = jax.vmap(lambda one: jax.random.permutation(one, ROWS))(block_keys)
    return orders.reshape(N).astype(jnp.int32)


def levels(stream_key, shape, pieces, smallest, high):
    loudness, own = 1.0, jax.random.fold_in(stream_key, 6)
    for axis_at, blocks in pieces:
        steps = jnp.exp(jax.random.uniform(jax.random.fold_in(own, axis_at), (blocks,), jnp.float32, smallest / len(pieces), high / len(pieces)))
        loudness = loudness * jnp.repeat(steps, shape[axis_at] // blocks).reshape([-1 if axis == axis_at else 1 for axis in range(len(shape))])
    return loudness


def gaussian(own_key, extent, spread, reach, cuts=(), held_as=jnp.bfloat16):
    result = jax.random.normal(own_key, extent, jnp.float32) * spread
    if len(cuts) > 0:
        result = levels(own_key, extent, cuts, -0.22, 0.18) * result
    return jnp.clip(result, min=-reach, max=reach).astype(held_as)


def setup_inputs(seed: int = 0) -> dict:
    keys = jax.random.split(jax.random.key(seed), 5)
    prompt_features = draw_prompt_features(jax.random.fold_in(keys[4], 71), 0)
    refusal_features = draw_refusal_features(jax.random.fold_in(keys[4], 71), 0)
    projection = gaussian(keys[2], (D, E), D ** -0.5, 0.1875, ((1, 8),))
    positives = draw_positives(jax.random.fold_in(keys[4], 71), 0)
    return {"prompt_features": prompt_features, "refusal_features": refusal_features, "projection": projection, "positives": positives}


def reference(prompt_features, refusal_features, projection, positives):
    inv_scale = E ** -0.5
    prompt_emb = jnp.dot(prompt_features, projection, preferred_element_type=jnp.float32).astype(jnp.bfloat16)
    refusal_emb = jnp.dot(refusal_features, projection, preferred_element_type=jnp.float32).astype(jnp.bfloat16)
    query_blocks = prompt_emb.reshape(N_DP, ROWS, E)
    pair_blocks = positives.reshape(N_DP, ROWS)
    block_starts = jnp.arange(N_DP, dtype=jnp.int32) * ROWS

    def first_pass(carry, query_block):
        col_top, col_total = carry
        scores = jnp.dot(query_block, refusal_emb.T, preferred_element_type=jnp.float32) * inv_scale
        row_top = jnp.max(scores, axis=1)
        row_lse = row_top + jnp.log(jnp.sum(jnp.exp(scores - row_top[:, None]), axis=1))
        new_top = jnp.maximum(col_top, jnp.max(scores, axis=0))
        col_total = col_total * jnp.exp(col_top - new_top) + jnp.sum(jnp.exp(scores - new_top[None, :]), axis=0)
        return (new_top, col_total), row_lse

    init = (jnp.full((N,), -jnp.inf, jnp.float32), jnp.zeros((N,), jnp.float32))
    (col_top, col_total), row_lse = lax.scan(first_pass, init, query_blocks)
    col_lse = col_top + jnp.log(col_total)
    key_index = jnp.arange(N, dtype=jnp.int32)

    def second_pass(key_grad, item):
        query_block, pair_block, start, lse_block = item
        scores = jnp.dot(query_block, refusal_emb.T, preferred_element_type=jnp.float32) * inv_scale
        marks = (key_index[None, :] == (start + pair_block)[:, None]).astype(jnp.float32)
        probs = (jnp.exp(scores - lse_block[:, None]) + jnp.exp(scores - col_lse[None, :])) - 2.0 * marks
        grads = (probs / (2.0 * N)).astype(jnp.bfloat16)
        prompt_part = jnp.dot(grads, refusal_emb, preferred_element_type=jnp.float32) * inv_scale
        key_grad = key_grad + jnp.dot(grads.T, query_block, preferred_element_type=jnp.float32) * inv_scale
        return key_grad, prompt_part

    key_grad, prompt_parts = lax.scan(second_pass, jnp.zeros((N, E), jnp.float32), (query_blocks, pair_blocks, block_starts, row_lse))
    prompt_grad = prompt_parts.reshape(N, E).astype(jnp.bfloat16)
    refusal_grad = key_grad.astype(jnp.bfloat16)
    return jnp.dot(prompt_features.T, prompt_grad, preferred_element_type=jnp.float32) + jnp.dot(refusal_features.T, refusal_grad, preferred_element_type=jnp.float32)
```

```python
import jax
import jax.numpy as jnp
from jax import lax
from jax.sharding import Mesh, PartitionSpec as P

DP = ("x_lo", "z", "core")
CUTS = ("y", "x_hi")
PLANE = ("core", "x_lo", "y", "x_hi")
SPREAD = ("x_lo", "y", "x_hi")


def exchange(x, axes):
    return lax.all_to_all(x, axes, split_axis=0, concat_axis=0, tiled=True)


def from_all(x, axes):
    return exchange(jnp.broadcast_to(x[None], (lax.axis_size(axes), *x.shape)), axes)


def from_twin(x, axis):
    return lax.ppermute(x, axis, [(0, 1), (1, 0)])


def from_ahead(x, axis, by):
    devices = lax.axis_size(axis)
    return lax.ppermute(x, axis, [((i + by) % devices, i) for i in range(devices)])


def in_order(mine, other, axis, dimension):
    first = lax.axis_index(axis) == 0
    return jnp.concatenate(
        [jnp.where(first, mine, other), jnp.where(first, other, mine)], dimension
    )


def whole_projection(projection):
    half = projection.shape[0] // 2
    own = lax.dynamic_slice_in_dim(projection, lax.axis_index("core") * half, half, 0)
    strip = in_order(own, from_twin(own, "x_hi"), "x_hi", 1)
    turns, at = lax.axis_size("y"), lax.axis_index("y")
    strips = [strip] + [from_ahead(strip, "y", by) for by in range(1, turns)]
    lap = jnp.concatenate(strips + strips, 1)
    start = (turns - at) % turns * strip.shape[1]
    mine = lax.dynamic_slice_in_dim(lap, start, turns * strip.shape[1], 1)
    return in_order(mine, from_twin(mine, "core"), "core", 0)


def log_sum_exp(x, axis):
    top = jnp.max(x, axis=axis, keepdims=True)
    total = jnp.sum(jnp.exp(x - top), axis=axis)
    return jnp.squeeze(top, axis) + jnp.log(total)


def own_first(x):
    x = jnp.where(lax.axis_index("core") == 1, x[::-1], x)
    return jnp.where(lax.axis_index("x_lo") == 1, x[:, ::-1], x)


def in_two(x):
    high = lax.reduce_precision(x, 8, 7)
    return high.astype(jnp.bfloat16), (x - high).astype(jnp.bfloat16)


def dot_first(a, b):
    return lax.dot_general(a, b, (((0,), (0,)), ((), ())), preferred_element_type=jnp.float32)


def shards(prompt_features, refusal_features, projection, positives):
    rows, depth = prompt_features.shape
    cuts = lax.axis_size(CUTS)
    width = projection.shape[1] * cuts
    pairs = rows * lax.axis_size(DP)
    inv_scale = width ** (-0.5)
    cut = lax.axis_index(CUTS)
    layer = lax.axis_index("z")
    chunk = rows // cuts

    own = lax.dynamic_slice_in_dim(refusal_features, cut * chunk, chunk, 0)
    refusals = from_all(own, "z").reshape(-1, depth)
    whole = whole_projection(projection)
    beside = from_twin(prompt_features, "x_lo")
    pair_of_shards = jnp.concatenate([prompt_features, beside], 0)
    prompts = jnp.concatenate([pair_of_shards, from_twin(pair_of_shards, "core")], 0)

    prompt_emb = jnp.dot(prompts, whole, preferred_element_type=jnp.float32).astype(jnp.bfloat16)
    refusal_emb = jnp.dot(refusals, whole, preferred_element_type=jnp.float32).astype(jnp.bfloat16)
    scores = (
        lax.dot_general(
            refusal_emb, prompt_emb, (((1,), (1,)), ((), ())), preferred_element_type=jnp.float32
        )
        * inv_scale
    )
    n_keys, n_queries = scores.shape

    col_part = log_sum_exp(scores, 1).reshape(-1, 128)
    col_lse = log_sum_exp(from_all(col_part, "z"), 0).reshape(n_keys)
    row_part = own_first(log_sum_exp(scores, 0).reshape(2, 2, rows)).reshape(-1, 128)
    row_part = log_sum_exp(from_all(row_part, PLANE), 0)
    row_lse = own_first(row_part.reshape(2, 2, rows)).reshape(n_queries)

    pair = jnp.concatenate([positives, jnp.full((n_queries - rows,), -1, jnp.int32)])
    key = jnp.arange(n_keys, dtype=jnp.int32)
    place = jnp.where(key // chunk == layer, cut * chunk + key % chunk, -2)
    marks = (pair[None, :] == place[:, None]).astype(jnp.float32)
    probs = jnp.exp(scores - row_lse[None, :]) + jnp.exp(scores - col_lse[:, None])
    grads = ((probs - 2.0 * marks) / (2.0 * pairs)).astype(jnp.bfloat16)

    prompt_grad = in_two(dot_first(grads, refusal_emb) * inv_scale)
    refusal_grad = in_two(
        jnp.dot(grads, prompt_emb, preferred_element_type=jnp.float32) * inv_scale
    )

    def product(start, count):
        left = lax.dynamic_slice_in_dim(prompts, start, count, 1)
        right = lax.dynamic_slice_in_dim(refusals, start, count, 1)
        return (
            dot_first(left, prompt_grad[0])
            + dot_first(right, refusal_grad[0])
            + (dot_first(left, prompt_grad[1]) + dot_first(right, refusal_grad[1]))
        )

    core = lax.axis_index("core")
    half = depth // 2
    came = from_twin(product((1 - core) * half, half), "core")
    kept = (product(core * half, half) + came).astype(jnp.bfloat16)
    parts = lax.axis_size("x_lo")
    pieces = kept.reshape(parts, half // parts, cuts, width // cuts).transpose(0, 2, 1, 3)
    pieces = pieces.reshape(parts * cuts, half // parts, width // cuts)
    in_layer = jnp.sum(exchange(pieces, SPREAD).astype(jnp.float32), axis=0)
    slices = in_layer.reshape(lax.axis_size("z"), -1, width // cuts)
    done = jnp.sum(exchange(slices, "z"), axis=0)
    block = from_all(done, "z").reshape(in_layer.shape)
    return lax.all_gather(block, ("core", "x_lo"), axis=0, tiled=True)


def solution(mesh):
    split = Mesh(mesh.devices.reshape(2, 16, 2, 4, 2), ("x_lo", "z", "core", "y", "x_hi"))
    placed = (P(DP, None), P(DP, None), P(None, CUTS), P(DP))
    return jax.shard_map(
        shards, mesh=split, in_specs=placed, out_specs=P(None, CUTS), check_vma=False
    )
```

```python
import jax
import jax.numpy as jnp
from jax import lax
from jax.experimental import pallas as pl
from jax.experimental.pallas import tpu as pltpu
from jax.sharding import Mesh, PartitionSpec as P

DP = ("x_lo", "z_hi", "z_lo", "core")
LAYERS = ("z_hi", "z_lo")
CUTS = ("y", "x_hi")
PLANE = ("core", "x_lo", "y", "x_hi")
SPREAD = ("x_lo", "y", "x_hi")


def exchange(x, axes):
    return lax.all_to_all(x, axes, split_axis=0, concat_axis=0, tiled=True)


def from_all(x, axes):
    return exchange(jnp.broadcast_to(x[None], (lax.axis_size(axes), *x.shape)), axes)


def from_twin(x, axis):
    return lax.ppermute(x, axis, [(0, 1), (1, 0)])


def from_ahead(x, axis, by):
    devices = lax.axis_size(axis)
    return lax.ppermute(x, axis, [((i + by) % devices, i) for i in range(devices)])


def in_order(mine, other, axis, dimension):
    first = lax.axis_index(axis) == 0
    return jnp.concatenate(
        [jnp.where(first, mine, other), jnp.where(first, other, mine)], dimension
    )


def projection_strip(projection):
    half = projection.shape[0] // 2
    own = lax.dynamic_slice_in_dim(projection, lax.axis_index("core") * half, half, 0)
    return in_order(own, from_twin(own, "x_hi"), "x_hi", 1)


def projection_halves(strip):
    strips = [strip] + [from_ahead(strip, "y", by) for by in range(1, lax.axis_size("y"))]
    near = jnp.stack(strips)
    return near, from_twin(near, "core")


def project_kernel(at_ref, x_ref, near_ref, far_ref, out_ref):
    turn, core = at_ref[0], at_ref[1]
    turns, half, wide = near_ref.shape
    near_x = x_ref[:, pl.ds(pl.multiple_of(core * half, half), half)]
    far_x = x_ref[:, pl.ds(pl.multiple_of((1 - core) * half, half), half)]
    for by in range(turns):
        block = jnp.dot(near_x, near_ref[by], preferred_element_type=jnp.float32)
        block += jnp.dot(far_x, far_ref[by], preferred_element_type=jnp.float32)
        place = pl.multiple_of(lax.rem(turn + by, turns) * wide, wide)
        out_ref[:, pl.ds(place, wide)] = block.astype(out_ref.dtype)


def project(x, near, far):
    rows, depth = x.shape
    width = near.shape[0] * near.shape[2]
    at = jnp.stack([lax.axis_index("y"), lax.axis_index("core")]).astype(jnp.int32)
    block = 256
    return pl.pallas_call(
        project_kernel,
        grid=(rows // block,),
        out_shape=jax.ShapeDtypeStruct((rows, width), jnp.bfloat16),
        in_specs=[
            pl.BlockSpec(memory_space=pltpu.SMEM),
            pl.BlockSpec((block, depth), lambda i: (i, 0)),
            pl.BlockSpec(near.shape, lambda i: (0, 0, 0)),
            pl.BlockSpec(far.shape, lambda i: (0, 0, 0)),
        ],
        out_specs=pl.BlockSpec((block, width), lambda i: (i, 0)),
        cost_estimate=pl.CostEstimate(
            flops=2 * rows * depth * width,
            bytes_accessed=2 * (rows * depth + depth * width + rows * width),
            transcendentals=0,
        ),
        compiler_params=pltpu.CompilerParams(vmem_limit_bytes=32 * 2**20),
    )(at, x, near, far)


def log_sum_exp(x, axis):
    top = jnp.max(x, axis=axis, keepdims=True)
    total = jnp.sum(jnp.exp(x - top), axis=axis)
    return jnp.squeeze(top, axis) + jnp.log(total)


def own_first(x):
    x = jnp.where(lax.axis_index("core") == 1, x[::-1], x)
    return jnp.where(lax.axis_index("x_lo") == 1, x[:, ::-1], x)


def in_two(x):
    high = lax.reduce_precision(x, 8, 7)
    return high.astype(jnp.bfloat16), (x - high).astype(jnp.bfloat16)


def dot_first(a, b):
    return lax.dot_general(a, b, (((0,), (0,)), ((), ())), preferred_element_type=jnp.float32)


def shards(prompt_features, refusal_features, projection, positives):
    rows, depth = prompt_features.shape
    cuts = lax.axis_size(CUTS)
    width = projection.shape[1] * cuts
    pairs = rows * lax.axis_size(DP)
    inv_scale = width ** (-0.5)
    cut = lax.axis_index(CUTS)
    chunk = rows // cuts

    own = lax.dynamic_slice_in_dim(refusal_features, cut * chunk, chunk, 0)
    refusals = from_all(own, LAYERS).reshape(-1, depth)

    strip = projection_strip(projection)
    strip, shard = lax.optimization_barrier((strip, prompt_features))
    beside = from_twin(shard, "x_lo")
    near, far = projection_halves(strip)
    pair_of_shards = jnp.concatenate([shard, beside], 0)
    prompts = jnp.concatenate([pair_of_shards, from_twin(pair_of_shards, "core")], 0)

    prompt_emb = project(prompts, near, far)
    refusal_emb = project(refusals, near, far)
    scores = (
        lax.dot_general(
            refusal_emb, prompt_emb, (((1,), (1,)), ((), ())), preferred_element_type=jnp.float32
        )
        * inv_scale
    )
    n_keys, n_queries = scores.shape

    col_part = log_sum_exp(scores, 1).reshape(-1, 128)
    row_part = own_first(log_sum_exp(scores, 0).reshape(2, 2, rows)).reshape(-1, 128)
    col_part, row_part, scores = lax.optimization_barrier((col_part, row_part, scores))
    cols = from_all(col_part, LAYERS)
    cols, row_part, scores, positives = lax.optimization_barrier(
        (cols, row_part, scores, positives)
    )
    all_rows = from_all(row_part, PLANE)
    cols, all_rows, scores, positives = lax.optimization_barrier(
        (cols, all_rows, scores, positives)
    )
    row_lse = own_first(log_sum_exp(all_rows, 0).reshape(2, 2, rows)).reshape(n_queries)
    col_lse = log_sum_exp(cols, 0).reshape(n_keys)

    pair = jnp.concatenate([positives, jnp.full((n_queries - rows,), -1, jnp.int32)])
    key = jnp.arange(n_keys, dtype=jnp.int32)
    place = jnp.where(key // chunk == lax.axis_index(LAYERS), cut * chunk + key % chunk, -2)
    marks = (pair[None, :] == place[:, None]).astype(jnp.float32)
    probs = jnp.exp(scores - row_lse[None, :]) + jnp.exp(scores - col_lse[:, None])
    grads = ((probs - 2.0 * marks) / (2.0 * pairs)).astype(jnp.bfloat16)

    grads = lax.optimization_barrier(grads)
    prompt_grad = in_two(dot_first(grads, refusal_emb) * inv_scale)
    refusal_grad = in_two(
        jnp.dot(grads, prompt_emb, preferred_element_type=jnp.float32) * inv_scale
    )

    def product(start, count):
        left = lax.dynamic_slice_in_dim(prompts, start, count, 1)
        right = lax.dynamic_slice_in_dim(refusals, start, count, 1)
        return (
            dot_first(left, prompt_grad[0])
            + dot_first(right, refusal_grad[0])
            + (dot_first(left, prompt_grad[1]) + dot_first(right, refusal_grad[1]))
        )

    core = lax.axis_index("core")
    half = depth // 2
    came = from_twin(product((1 - core) * half, half), "core")
    kept = (product(core * half, half) + came).astype(jnp.bfloat16)
    parts = lax.axis_size("x_lo")
    pieces = kept.reshape(parts, half // parts, cuts, width // cuts).transpose(0, 2, 1, 3)
    pieces = pieces.reshape(parts * cuts, half // parts, width // cuts)
    in_layer = jnp.sum(exchange(pieces, SPREAD).astype(jnp.float32), axis=0)
    slices = in_layer.reshape(lax.axis_size(LAYERS), -1, width // cuts)
    done = jnp.sum(exchange(slices, LAYERS), axis=0)
    block = from_all(done, LAYERS).reshape(in_layer.shape)
    return from_all(block, ("core", "x_lo")).reshape(depth, width // cuts)


def solution(mesh):
    split = Mesh(
        mesh.devices.reshape(2, 4, 4, 2, 4, 2), ("x_lo", "z_hi", "z_lo", "core", "y", "x_hi")
    )
    placed = (P(DP, None), P(DP, None), P(None, CUTS), P(DP))
    return jax.shard_map(
        shards, mesh=split, in_specs=placed, out_specs=P(None, CUTS), check_vma=False
    )
```

```python
import jax
import jax.numpy as jnp
from jax import lax
from jax.experimental import pallas as pl
from jax.experimental.pallas import tpu as pltpu
from jax.sharding import Mesh, PartitionSpec as P

DP = ("x_lo", "z_hi", "z_lo", "core")
LAYERS = ("z_hi", "z_lo")
CUTS = ("y", "x_hi")
PLANE = ("core", "x_lo", "y", "x_hi")
SPREAD = ("x_lo", "y", "x_hi")


def exchange(x, axes):
    return lax.all_to_all(x, axes, split_axis=0, concat_axis=0, tiled=True)


def from_all(x, axes):
    return exchange(jnp.broadcast_to(x[None], (lax.axis_size(axes), *x.shape)), axes)


def from_twin(x, axis):
    return lax.ppermute(x, axis, [(0, 1), (1, 0)])


def from_ahead(x, axis, by):
    devices = lax.axis_size(axis)
    return lax.ppermute(x, axis, [((i + by) % devices, i) for i in range(devices)])


def in_order(mine, other, axis, dimension):
    first = lax.axis_index(axis) == 0
    return jnp.concatenate(
        [jnp.where(first, mine, other), jnp.where(first, other, mine)], dimension
    )


def projection_strip(projection):
    half = projection.shape[0] // 2
    own = lax.dynamic_slice_in_dim(projection, lax.axis_index("core") * half, half, 0)
    return in_order(own, from_twin(own, "x_hi"), "x_hi", 1)


def projection_halves(strip):
    strips = [strip] + [from_ahead(strip, "y", by) for by in range(1, lax.axis_size("y"))]
    near = jnp.stack(strips)
    return near, from_twin(near, "core")


def project_kernel(at_ref, x_ref, near_ref, far_ref, out_ref):
    turn, core = at_ref[0], at_ref[1]
    turns, half, wide = near_ref.shape
    near_x = x_ref[:, pl.ds(pl.multiple_of(core * half, half), half)]
    far_x = x_ref[:, pl.ds(pl.multiple_of((1 - core) * half, half), half)]
    for by in range(turns):
        block = jnp.dot(near_x, near_ref[by], preferred_element_type=jnp.float32)
        block += jnp.dot(far_x, far_ref[by], preferred_element_type=jnp.float32)
        place = pl.multiple_of(lax.rem(turn + by, turns) * wide, wide)
        out_ref[:, pl.ds(place, wide)] = block.astype(out_ref.dtype)


def project(x, near, far):
    rows, depth = x.shape
    width = near.shape[0] * near.shape[2]
    at = jnp.stack([lax.axis_index("y"), lax.axis_index("core")]).astype(jnp.int32)
    block = 256
    return pl.pallas_call(
        project_kernel,
        grid=(rows // block,),
        out_shape=jax.ShapeDtypeStruct((rows, width), jnp.bfloat16),
        in_specs=[
            pl.BlockSpec(memory_space=pltpu.SMEM),
            pl.BlockSpec((block, depth), lambda i: (i, 0)),
            pl.BlockSpec(near.shape, lambda i: (0, 0, 0)),
            pl.BlockSpec(far.shape, lambda i: (0, 0, 0)),
        ],
        out_specs=pl.BlockSpec((block, width), lambda i: (i, 0)),
        cost_estimate=pl.CostEstimate(
            flops=2 * rows * depth * width,
            bytes_accessed=2 * (rows * depth + depth * width + rows * width),
            transcendentals=0,
        ),
        compiler_params=pltpu.CompilerParams(vmem_limit_bytes=12 * 2**20),
    )(at, x, near, far)


def log_sum_exp(x, axis):
    top = jnp.max(x, axis=axis, keepdims=True)
    total = jnp.sum(jnp.exp(x - top), axis=axis)
    return jnp.squeeze(top, axis) + jnp.log(total)


def own_first(x):
    x = jnp.where(lax.axis_index("core") == 1, x[::-1], x)
    return jnp.where(lax.axis_index("x_lo") == 1, x[:, ::-1], x)


def in_two(x):
    high = lax.reduce_precision(x, 8, 7)
    return high.astype(jnp.bfloat16), (x - high).astype(jnp.bfloat16)


def dot_first(a, b):
    return lax.dot_general(a, b, (((0,), (0,)), ((), ())), preferred_element_type=jnp.float32)


def score(refusal_emb, prompt_emb, inv_scale):
    return inv_scale * lax.dot_general(
        refusal_emb, prompt_emb, (((1,), (1,)), ((), ())), preferred_element_type=jnp.float32
    )


def shards(prompt_features, refusal_features, projection, positives):
    rows, depth = prompt_features.shape
    cuts = lax.axis_size(CUTS)
    width = projection.shape[1] * cuts
    pairs = rows * lax.axis_size(DP)
    inv_scale = width ** (-0.5)
    cut = lax.axis_index(CUTS)
    chunk = rows // cuts

    own = lax.dynamic_slice_in_dim(refusal_features, cut * chunk, chunk, 0)
    refusals = from_all(own, LAYERS).reshape(-1, depth)

    strip = projection_strip(projection)
    strip, shard = lax.optimization_barrier((strip, prompt_features))
    beside = from_twin(shard, "x_lo")
    near, far = projection_halves(strip)
    pair_of_shards = jnp.concatenate([shard, beside], 0)
    prompts = jnp.concatenate([pair_of_shards, from_twin(pair_of_shards, "core")], 0)

    prompt_emb = project(prompts, near, far)
    refusal_emb = project(refusals, near, far)
    scores = score(refusal_emb, prompt_emb, inv_scale)
    n_keys, n_queries = scores.shape

    col_part = log_sum_exp(scores, 1).reshape(-1, 128)
    row_part = own_first(log_sum_exp(scores, 0).reshape(2, 2, rows)).reshape(-1, 128)
    col_part, row_part = lax.optimization_barrier((col_part, row_part))
    cols = from_all(col_part, LAYERS)
    cols, row_part, positives = lax.optimization_barrier((cols, row_part, positives))
    all_rows = from_all(row_part, PLANE)
    cols, all_rows, positives, refusal_emb = lax.optimization_barrier(
        (cols, all_rows, positives, refusal_emb)
    )
    row_lse = own_first(log_sum_exp(all_rows, 0).reshape(2, 2, rows)).reshape(n_queries)
    col_lse = log_sum_exp(cols, 0).reshape(n_keys)

    pair = jnp.concatenate([positives, jnp.full((n_queries - rows,), -1, jnp.int32)])
    key = jnp.arange(n_keys, dtype=jnp.int32)
    place = jnp.where(key // chunk == lax.axis_index(LAYERS), cut * chunk + key % chunk, -2)
    marks = (pair[None, :] == place[:, None]).astype(jnp.float32)
    scores = score(refusal_emb, prompt_emb, inv_scale)
    probs = jnp.exp(scores - row_lse[None, :]) + jnp.exp(scores - col_lse[:, None])
    grads = ((probs - 2.0 * marks) / (2.0 * pairs)).astype(jnp.bfloat16)
    grads = lax.optimization_barrier(grads)

    prompt_sum = in_two(jnp.dot(grads, prompts, preferred_element_type=jnp.float32) * inv_scale)
    refusal_grad = in_two(
        jnp.dot(grads, prompt_emb, preferred_element_type=jnp.float32) * inv_scale
    )

    def product(start, count):
        right = lax.dynamic_slice_in_dim(refusals, start, count, 1)
        left = [lax.dynamic_slice_in_dim(x, start, count, 1) for x in prompt_sum]
        return (
            dot_first(left[0], refusal_emb)
            + dot_first(right, refusal_grad[0])
            + (dot_first(left[1], refusal_emb) + dot_first(right, refusal_grad[1]))
        )

    core = lax.axis_index("core")
    half = depth // 2
    came = from_twin(product((1 - core) * half, half), "core")
    kept = (product(core * half, half) + came).astype(jnp.bfloat16)
    parts = lax.axis_size("x_lo")
    pieces = kept.reshape(parts, half // parts, cuts, width // cuts).transpose(0, 2, 1, 3)
    pieces = pieces.reshape(parts * cuts, half // parts, width // cuts)
    in_layer = jnp.sum(exchange(pieces, SPREAD).astype(jnp.float32), axis=0)
    slices = in_layer.reshape(lax.axis_size(LAYERS), -1, width // cuts)
    done = jnp.sum(exchange(slices, LAYERS), axis=0)
    block = from_all(done, LAYERS).reshape(in_layer.shape)
    return from_all(block, ("core", "x_lo")).reshape(depth, width // cuts)


def solution(mesh):
    split = Mesh(
        mesh.devices.reshape(2, 4, 4, 2, 4, 2), ("x_lo", "z_hi", "z_lo", "core", "y", "x_hi")
    )
    placed = (P(DP, None), P(DP, None), P(None, CUTS), P(DP))
    return jax.shard_map(
        shards, mesh=split, in_specs=placed, out_specs=P(None, CUTS), check_vma=False
    )
```

```python
import jax
import jax.numpy as jnp
from jax import lax
from jax.experimental import pallas as pl
from jax.experimental.pallas import tpu as pltpu
from jax.sharding import Mesh, PartitionSpec as P

DP = ("x_lo", "z_hi", "z_lo", "core")
LAYERS = ("z_hi", "z_lo")
CUTS = ("y", "x_hi")
PLANE = ("core", "x_lo", "y", "x_hi")
SPREAD = ("x_lo", "y", "x_hi")


def exchange(x, axes):
    return lax.all_to_all(x, axes, split_axis=0, concat_axis=0, tiled=True)


def from_all(x, axes):
    return exchange(jnp.broadcast_to(x[None], (lax.axis_size(axes), *x.shape)), axes)


def from_twin(x, axis):
    return lax.ppermute(x, axis, [(0, 1), (1, 0)])


def from_ahead(x, axis, by):
    devices = lax.axis_size(axis)
    return lax.ppermute(x, axis, [((i + by) % devices, i) for i in range(devices)])


def in_order(mine, other, axis, dimension):
    first = lax.axis_index(axis) == 0
    return jnp.concatenate(
        [jnp.where(first, mine, other), jnp.where(first, other, mine)], dimension
    )


def projection_strip(projection):
    half = projection.shape[0] // 2
    own = lax.dynamic_slice_in_dim(projection, lax.axis_index("core") * half, half, 0)
    return in_order(own, from_twin(own, "x_hi"), "x_hi", 1)


def projection_halves(strip):
    strips = [strip] + [from_ahead(strip, "y", by) for by in range(1, lax.axis_size("y"))]
    near = jnp.stack(strips)
    return near, from_twin(near, "core")


def project_kernel(at_ref, x_ref, near_ref, far_ref, out_ref):
    turn, core = at_ref[0], at_ref[1]
    turns, half, wide = near_ref.shape
    near_x = x_ref[:, pl.ds(pl.multiple_of(core * half, half), half)]
    far_x = x_ref[:, pl.ds(pl.multiple_of((1 - core) * half, half), half)]
    for by in range(turns):
        block = jnp.dot(near_x, near_ref[by], preferred_element_type=jnp.float32)
        block += jnp.dot(far_x, far_ref[by], preferred_element_type=jnp.float32)
        place = pl.multiple_of(lax.rem(turn + by, turns) * wide, wide)
        out_ref[:, pl.ds(place, wide)] = block.astype(out_ref.dtype)


def project(x, near, far):
    rows, depth = x.shape
    width = near.shape[0] * near.shape[2]
    at = jnp.stack([lax.axis_index("y"), lax.axis_index("core")]).astype(jnp.int32)
    block = 256
    return pl.pallas_call(
        project_kernel,
        grid=(rows // block,),
        out_shape=jax.ShapeDtypeStruct((rows, width), jnp.bfloat16),
        in_specs=[
            pl.BlockSpec(memory_space=pltpu.SMEM),
            pl.BlockSpec((block, depth), lambda i: (i, 0)),
            pl.BlockSpec(near.shape, lambda i: (0, 0, 0)),
            pl.BlockSpec(far.shape, lambda i: (0, 0, 0)),
        ],
        out_specs=pl.BlockSpec((block, width), lambda i: (i, 0)),
        cost_estimate=pl.CostEstimate(
            flops=2 * rows * depth * width,
            bytes_accessed=2 * (rows * depth + depth * width + rows * width),
            transcendentals=0,
        ),
        compiler_params=pltpu.CompilerParams(vmem_limit_bytes=8 * 2**20),
    )(at, x, near, far)


def log_sum_exp(x, axis):
    top = jnp.max(x, axis=axis, keepdims=True)
    total = jnp.sum(jnp.exp(x - top), axis=axis)
    return jnp.squeeze(top, axis) + jnp.log(total)


def own_first(x):
    x = jnp.where(lax.axis_index("core") == 1, x[::-1], x)
    return jnp.where(lax.axis_index("x_lo") == 1, x[:, ::-1], x)


def in_two(x):
    high = lax.reduce_precision(x, 8, 7)
    return high.astype(jnp.bfloat16), (x - high).astype(jnp.bfloat16)


def dot_first(a, b):
    return lax.dot_general(a, b, (((0,), (0,)), ((), ())), preferred_element_type=jnp.float32)


def score(refusal_emb, prompt_emb, inv_scale):
    return inv_scale * lax.dot_general(
        refusal_emb, prompt_emb, (((1,), (1,)), ((), ())), preferred_element_type=jnp.float32
    )


def shards(prompt_features, refusal_features, projection, positives):
    rows, depth = prompt_features.shape
    cuts = lax.axis_size(CUTS)
    width = projection.shape[1] * cuts
    pairs = rows * lax.axis_size(DP)
    inv_scale = width ** (-0.5)
    cut = lax.axis_index(CUTS)
    chunk = rows // cuts

    own = lax.dynamic_slice_in_dim(refusal_features, cut * chunk, chunk, 0)
    refusals = from_all(own, LAYERS).reshape(-1, depth)

    strip = projection_strip(projection)
    strip, shard = lax.optimization_barrier((strip, prompt_features))
    beside = from_twin(shard, "x_lo")
    near, far = projection_halves(strip)
    pair_of_shards = jnp.concatenate([shard, beside], 0)
    prompts = jnp.concatenate([pair_of_shards, from_twin(pair_of_shards, "core")], 0)

    prompt_emb = project(prompts, near, far)
    refusal_emb = project(refusals, near, far)
    scores = score(refusal_emb, prompt_emb, inv_scale)
    n_keys, n_queries = scores.shape

    col_part = log_sum_exp(scores, 1).reshape(-1, 128)
    row_part = own_first(log_sum_exp(scores, 0).reshape(2, 2, rows)).reshape(-1, 128)
    col_part, row_part = lax.optimization_barrier((col_part, row_part))
    core = lax.axis_index("core")
    half = depth // 2
    given, own = ((1 - core) * half).astype(jnp.uint32), (core * half).astype(jnp.uint32)
    layer, start = lax.axis_index(LAYERS), cut * chunk

    all_rows = from_all(row_part, PLANE)
    places = (given + 2 * own).astype(jnp.float32) + (layer + start).astype(jnp.float32)
    cols = from_all(col_part + 0.0 * places, LAYERS)
    cols, all_rows, positives, refusal_emb = lax.optimization_barrier(
        (cols, all_rows, positives, refusal_emb)
    )
    row_lse = own_first(log_sum_exp(all_rows, 0).reshape(2, 2, rows)).reshape(n_queries)
    col_lse = log_sum_exp(cols, 0).reshape(n_keys)

    pair = jnp.concatenate([positives, jnp.full((n_queries - rows,), -1, jnp.int32)])
    key = jnp.arange(n_keys, dtype=jnp.int32) + (0.0 * col_lse).astype(jnp.int32)
    place = jnp.where(key // chunk == layer, start + key % chunk, -2)
    marks = (pair[None, :] == place[:, None]).astype(jnp.float32)
    scores = score(refusal_emb, prompt_emb, inv_scale)
    probs = jnp.exp(scores - row_lse[None, :]) + jnp.exp(scores - col_lse[:, None])
    grads = ((probs - 2.0 * marks) / (2.0 * pairs)).astype(jnp.bfloat16)
    grads = lax.optimization_barrier(grads)

    prompt_sum = in_two(jnp.dot(grads, prompts, preferred_element_type=jnp.float32) * inv_scale)
    refusal_grad = in_two(
        jnp.dot(grads, prompt_emb, preferred_element_type=jnp.float32) * inv_scale
    )

    def product(start, count):
        right = lax.dynamic_slice_in_dim(refusals, start, count, 1)
        left = [lax.dynamic_slice_in_dim(x, start, count, 1) for x in prompt_sum]
        return (
            dot_first(left[0], refusal_emb)
            + dot_first(right, refusal_grad[0])
            + (dot_first(left[1], refusal_emb) + dot_first(right, refusal_grad[1]))
        )

    came = from_twin(product(given, half), "core")
    kept = (product(own, half) + came).astype(jnp.bfloat16)
    parts = lax.axis_size("x_lo")
    pieces = kept.reshape(parts, half // parts, cuts, width // cuts).transpose(0, 2, 1, 3)
    pieces = pieces.reshape(parts * cuts, half // parts, width // cuts)
    in_layer = jnp.sum(exchange(pieces, SPREAD).astype(jnp.float32), axis=0)
    slices = in_layer.reshape(lax.axis_size(LAYERS), -1, width // cuts)
    done = jnp.sum(exchange(slices, LAYERS), axis=0)
    block = from_all(done, LAYERS).reshape(in_layer.shape)
    return from_all(block, ("core", "x_lo")).reshape(depth, width // cuts)


def solution(mesh):
    split = Mesh(
        mesh.devices.reshape(2, 4, 4, 2, 4, 2), ("x_lo", "z_hi", "z_lo", "core", "y", "x_hi")
    )
    placed = (P(DP, None), P(DP, None), P(None, CUTS), P(DP))
    return jax.shard_map(
        shards, mesh=split, in_specs=placed, out_specs=P(None, CUTS), check_vma=False
    )
```

```python
import jax
import jax.numpy as jnp
from jax import lax
from jax.experimental import pallas as pl
from jax.experimental.pallas import tpu as pltpu
from jax.sharding import Mesh, PartitionSpec as P

DP = ("x_lo", "z_hi", "z_lo", "core")
LAYERS = ("z_hi", "z_lo")
CUTS = ("y", "x_hi")
PLANE = ("core", "x_lo", "y", "x_hi")
SPREAD = ("x_lo", "y", "x_hi")


def exchange(x, axes):
    return lax.all_to_all(x, axes, split_axis=0, concat_axis=0, tiled=True)


def from_all(x, axes):
    return exchange(jnp.broadcast_to(x[None], (lax.axis_size(axes), *x.shape)), axes)


def from_twin(x, axis):
    return lax.ppermute(x, axis, [(0, 1), (1, 0)])


def from_ahead(x, axis, by):
    devices = lax.axis_size(axis)
    return lax.ppermute(x, axis, [((i + by) % devices, i) for i in range(devices)])


def in_order(mine, other, axis, dimension):
    first = lax.axis_index(axis) == 0
    return jnp.concatenate(
        [jnp.where(first, mine, other), jnp.where(first, other, mine)], dimension
    )


def projection_strip(projection):
    half = projection.shape[0] // 2
    own = lax.dynamic_slice_in_dim(projection, lax.axis_index("core") * half, half, 0)
    return in_order(own, from_twin(own, "x_hi"), "x_hi", 1)


def projection_halves(strip):
    strips = [strip] + [from_ahead(strip, "y", by) for by in range(1, lax.axis_size("y"))]
    near = jnp.stack(strips)
    return near, from_twin(near, "core")


def project_kernel(at_ref, x_ref, near_ref, far_ref, out_ref):
    turn, core = at_ref[0], at_ref[1]
    turns, half, wide = near_ref.shape
    near_x = x_ref[:, pl.ds(pl.multiple_of(core * half, half), half)]
    far_x = x_ref[:, pl.ds(pl.multiple_of((1 - core) * half, half), half)]
    for by in range(turns):
        block = jnp.dot(near_x, near_ref[by], preferred_element_type=jnp.float32)
        block += jnp.dot(far_x, far_ref[by], preferred_element_type=jnp.float32)
        place = pl.multiple_of(lax.rem(turn + by, turns) * wide, wide)
        out_ref[:, pl.ds(place, wide)] = block.astype(out_ref.dtype)


def project(x, near, far):
    rows, depth = x.shape
    width = near.shape[0] * near.shape[2]
    at = jnp.stack([lax.axis_index("y"), lax.axis_index("core")]).astype(jnp.int32)
    block = 256
    return pl.pallas_call(
        project_kernel,
        grid=(rows // block,),
        out_shape=jax.ShapeDtypeStruct((rows, width), jnp.bfloat16),
        in_specs=[
            pl.BlockSpec(memory_space=pltpu.SMEM),
            pl.BlockSpec((block, depth), lambda i: (i, 0)),
            pl.BlockSpec(near.shape, lambda i: (0, 0, 0)),
            pl.BlockSpec(far.shape, lambda i: (0, 0, 0)),
        ],
        out_specs=pl.BlockSpec((block, width), lambda i: (i, 0)),
        cost_estimate=pl.CostEstimate(
            flops=2 * rows * depth * width,
            bytes_accessed=2 * (rows * depth + depth * width + rows * width),
            transcendentals=0,
        ),
        compiler_params=pltpu.CompilerParams(vmem_limit_bytes=8 * 2**20),
    )(at, x, near, far)


def log_sum_exp(x, axis):
    top = jnp.max(x, axis=axis, keepdims=True)
    total = jnp.sum(jnp.exp(x - top), axis=axis)
    return jnp.squeeze(top, axis) + jnp.log(total)


def own_first(x):
    x = jnp.where(lax.axis_index("core") == 1, x[::-1], x)
    return jnp.where(lax.axis_index("x_lo") == 1, x[:, ::-1], x)


def in_two(x):
    high = lax.reduce_precision(x, 8, 7)
    return high.astype(jnp.bfloat16), (x - high).astype(jnp.bfloat16)


def dot_first(a, b):
    return lax.dot_general(a, b, (((0,), (0,)), ((), ())), preferred_element_type=jnp.float32)


def score(refusal_emb, prompt_emb, inv_scale):
    return inv_scale * lax.dot_general(
        refusal_emb, prompt_emb, (((1,), (1,)), ((), ())), preferred_element_type=jnp.float32
    )


def shards(prompt_features, refusal_features, projection, positives):
    rows, depth = prompt_features.shape
    cuts = lax.axis_size(CUTS)
    width = projection.shape[1] * cuts
    pairs = rows * lax.axis_size(DP)
    inv_scale = width ** (-0.5)
    cut = lax.axis_index(CUTS)
    chunk = rows // cuts

    own = lax.dynamic_slice_in_dim(refusal_features, cut * chunk, chunk, 0)
    refusals = from_all(own, LAYERS).reshape(-1, depth)

    strip = projection_strip(projection)
    strip, shard = lax.optimization_barrier((strip, prompt_features))
    beside = from_twin(shard, "x_lo")
    near, far = projection_halves(strip)
    pair_of_shards = jnp.concatenate([shard, beside], 0)
    prompts = jnp.concatenate([pair_of_shards, from_twin(pair_of_shards, "core")], 0)

    prompt_emb = project(prompts, near, far)
    near = pltpu.with_memory_space_constraint(near, pltpu.HBM)
    far = pltpu.with_memory_space_constraint(far, pltpu.HBM)
    refusal_emb = project(refusals, near, far)
    scores = score(refusal_emb, prompt_emb, inv_scale)
    n_keys, n_queries = scores.shape

    col_part = log_sum_exp(scores, 1).reshape(-1, 128)
    row_part = own_first(log_sum_exp(scores, 0).reshape(2, 2, rows)).reshape(-1, 128)
    col_part, row_part = lax.optimization_barrier((col_part, row_part))
    core = lax.axis_index("core")
    half = depth // 2
    given, own = ((1 - core) * half).astype(jnp.uint32), (core * half).astype(jnp.uint32)
    layer, start = lax.axis_index(LAYERS), cut * chunk

    all_rows = from_all(row_part, PLANE)
    places = (given + 2 * own).astype(jnp.float32) + (layer + start).astype(jnp.float32)
    cols = from_all(col_part + 0.0 * places, LAYERS)
    cols, all_rows, positives, refusal_emb = lax.optimization_barrier(
        (cols, all_rows, positives, refusal_emb)
    )
    row_lse = own_first(log_sum_exp(all_rows, 0).reshape(2, 2, rows)).reshape(n_queries)
    col_lse = log_sum_exp(cols, 0).reshape(n_keys)

    pair = jnp.concatenate([positives, jnp.full((n_queries - rows,), -1, jnp.int32)])
    key = jnp.arange(n_keys, dtype=jnp.int32) + (0.0 * col_lse).astype(jnp.int32)
    place = jnp.where(key // chunk == layer, start + key % chunk, -2)
    marks = (pair[None, :] == place[:, None]).astype(jnp.float32)
    scores = score(refusal_emb, prompt_emb, inv_scale)
    probs = jnp.exp(scores - row_lse[None, :]) + jnp.exp(scores - col_lse[:, None])
    grads = ((probs - 2.0 * marks) / (2.0 * pairs)).astype(jnp.bfloat16)
    grads = lax.optimization_barrier(grads)

    prompt_sum = in_two(jnp.dot(grads, prompts, preferred_element_type=jnp.float32) * inv_scale)
    refusal_grad = in_two(
        jnp.dot(grads, prompt_emb, preferred_element_type=jnp.float32) * inv_scale
    )

    def product(start, count):
        right = lax.dynamic_slice_in_dim(refusals, start, count, 1)
        left = [lax.dynamic_slice_in_dim(x, start, count, 1) for x in prompt_sum]
        return (
            dot_first(left[0], refusal_emb)
            + dot_first(right, refusal_grad[0])
            + (dot_first(left[1], refusal_emb) + dot_first(right, refusal_grad[1]))
        )

    came = from_twin(product(given, half), "core")
    kept = (product(own, half) + came).astype(jnp.bfloat16)
    parts = lax.axis_size("x_lo")
    pieces = kept.reshape(parts, half // parts, cuts, width // cuts).transpose(0, 2, 1, 3)
    pieces = pieces.reshape(parts * cuts, half // parts, width // cuts)
    in_layer = jnp.sum(exchange(pieces, SPREAD).astype(jnp.float32), axis=0)
    slices = in_layer.reshape(lax.axis_size(LAYERS), -1, width // cuts)
    done = jnp.sum(exchange(slices, LAYERS), axis=0)
    block = from_all(done, LAYERS).reshape(in_layer.shape)
    return from_all(block, ("core", "x_lo")).reshape(depth, width // cuts)


def solution(mesh):
    split = Mesh(
        mesh.devices.reshape(2, 4, 4, 2, 4, 2), ("x_lo", "z_hi", "z_lo", "core", "y", "x_hi")
    )
    placed = (P(DP, None), P(DP, None), P(None, CUTS), P(DP))
    return jax.shard_map(
        shards, mesh=split, in_specs=placed, out_specs=P(None, CUTS), check_vma=False
    )
```

```python
import jax
import jax.numpy as jnp
from jax import lax
from jax.experimental import pallas as pl
from jax.experimental.pallas import tpu as pltpu
from jax.sharding import Mesh, PartitionSpec as P

DP = ("x_lo", "z_hi", "z_lo", "core")
LAYERS = ("z_hi", "z_lo")
CUTS = ("y", "x_hi")
PLANE = ("core", "x_lo", "y", "x_hi")
SPREAD = ("x_lo", "y", "x_hi")


def exchange(x, axes):
    return lax.all_to_all(x, axes, split_axis=0, concat_axis=0, tiled=True)


def from_all(x, axes):
    return exchange(jnp.broadcast_to(x[None], (lax.axis_size(axes), *x.shape)), axes)


def from_twin(x, axis):
    return lax.ppermute(x, axis, [(0, 1), (1, 0)])


def from_ahead(x, axis, by):
    devices = lax.axis_size(axis)
    return lax.ppermute(x, axis, [((i + by) % devices, i) for i in range(devices)])


def in_order(mine, other, axis, dimension):
    first = lax.axis_index(axis) == 0
    return jnp.concatenate(
        [jnp.where(first, mine, other), jnp.where(first, other, mine)], dimension
    )


def projection_strip(projection):
    half = projection.shape[0] // 2
    own = lax.dynamic_slice_in_dim(projection, lax.axis_index("core") * half, half, 0)
    return in_order(own, from_twin(own, "x_hi"), "x_hi", 1)


def projection_halves(strip):
    strips = [strip] + [from_ahead(strip, "y", by) for by in range(1, lax.axis_size("y"))]
    near = jnp.stack(strips)
    return near, from_twin(near, "core")


def project_kernel(at_ref, x_ref, near_ref, far_ref, out_ref):
    turn, core = at_ref[0], at_ref[1]
    turns, half, wide = near_ref.shape
    near_x = x_ref[:, pl.ds(pl.multiple_of(core * half, half), half)]
    far_x = x_ref[:, pl.ds(pl.multiple_of((1 - core) * half, half), half)]
    for by in range(turns):
        block = jnp.dot(near_x, near_ref[by], preferred_element_type=jnp.float32)
        block += jnp.dot(far_x, far_ref[by], preferred_element_type=jnp.float32)
        place = pl.multiple_of(lax.rem(turn + by, turns) * wide, wide)
        out_ref[:, pl.ds(place, wide)] = block.astype(out_ref.dtype)


def project(x, near, far):
    rows, depth = x.shape
    width = near.shape[0] * near.shape[2]
    at = jnp.stack([lax.axis_index("y"), lax.axis_index("core")]).astype(jnp.int32)
    block = 512
    return pl.pallas_call(
        project_kernel,
        grid=(rows // block,),
        out_shape=jax.ShapeDtypeStruct((rows, width), jnp.bfloat16),
        in_specs=[
            pl.BlockSpec(memory_space=pltpu.SMEM),
            pl.BlockSpec((block, depth), lambda i: (i, 0)),
            pl.BlockSpec(near.shape, lambda i: (0, 0, 0)),
            pl.BlockSpec(far.shape, lambda i: (0, 0, 0)),
        ],
        out_specs=pl.BlockSpec((block, width), lambda i: (i, 0)),
        cost_estimate=pl.CostEstimate(
            flops=2 * rows * depth * width,
            bytes_accessed=2 * (rows * depth + depth * width + rows * width),
            transcendentals=0,
        ),
        compiler_params=pltpu.CompilerParams(vmem_limit_bytes=14 * 2**20),
    )(at, x, near, far)


def log_sum_exp(x, axis):
    top = jnp.max(x, axis=axis, keepdims=True)
    total = jnp.sum(jnp.exp(x - top), axis=axis)
    return jnp.squeeze(top, axis) + jnp.log(total)


def own_first(x):
    x = jnp.where(lax.axis_index("core") == 1, x[::-1], x)
    return jnp.where(lax.axis_index("x_lo") == 1, x[:, ::-1], x)


def in_two(x):
    high = lax.reduce_precision(x, 8, 7)
    return high.astype(jnp.bfloat16), (x - high).astype(jnp.bfloat16)


def dot_first(a, b):
    return lax.dot_general(a, b, (((0,), (0,)), ((), ())), preferred_element_type=jnp.float32)


def score(refusal_emb, prompt_emb, inv_scale):
    return inv_scale * lax.dot_general(
        refusal_emb, prompt_emb, (((1,), (1,)), ((), ())), preferred_element_type=jnp.float32
    )


def shards(prompt_features, refusal_features, projection, positives):
    rows, depth = prompt_features.shape
    cuts = lax.axis_size(CUTS)
    width = projection.shape[1] * cuts
    pairs = rows * lax.axis_size(DP)
    inv_scale = width ** (-0.5)
    cut = lax.axis_index(CUTS)
    chunk = rows // cuts

    own = lax.dynamic_slice_in_dim(refusal_features, cut * chunk, chunk, 0)
    refusals = from_all(own, LAYERS).reshape(-1, depth)

    strip = projection_strip(projection)
    strip, shard = lax.optimization_barrier((strip, prompt_features))
    beside = from_twin(shard, "x_lo")
    near, far = projection_halves(strip)
    pair_of_shards = jnp.concatenate([shard, beside], 0)
    prompts = jnp.concatenate([pair_of_shards, from_twin(pair_of_shards, "core")], 0)

    prompt_emb = project(prompts, near, far)
    near = pltpu.with_memory_space_constraint(near, pltpu.HBM)
    far = pltpu.with_memory_space_constraint(far, pltpu.HBM)
    refusal_emb = project(refusals, near, far)
    scores = score(refusal_emb, prompt_emb, inv_scale)
    n_keys, n_queries = scores.shape

    col_part = log_sum_exp(scores, 1).reshape(-1, 128)
    row_part = own_first(log_sum_exp(scores, 0).reshape(2, 2, rows)).reshape(-1, 128)
    col_part, row_part = lax.optimization_barrier((col_part, row_part))
    core = lax.axis_index("core")
    half = depth // 2
    given, own = ((1 - core) * half).astype(jnp.uint32), (core * half).astype(jnp.uint32)
    layer, start = lax.axis_index(LAYERS), cut * chunk

    all_rows = from_all(row_part, PLANE)
    places = (given + 2 * own).astype(jnp.float32) + (layer + start).astype(jnp.float32)
    cols = from_all(col_part + 0.0 * places, LAYERS)
    cols, all_rows, positives, refusal_emb = lax.optimization_barrier(
        (cols, all_rows, positives, refusal_emb)
    )
    row_lse = own_first(log_sum_exp(all_rows, 0).reshape(2, 2, rows)).reshape(n_queries)
    col_lse = log_sum_exp(cols, 0).reshape(n_keys)

    pair = jnp.concatenate([positives, jnp.full((n_queries - rows,), -1, jnp.int32)])
    key = jnp.arange(n_keys, dtype=jnp.int32) + (0.0 * col_lse).astype(jnp.int32)
    place = jnp.where(key // chunk == layer, start + key % chunk, -2)
    marks = (pair[None, :] == place[:, None]).astype(jnp.float32)
    scores = score(refusal_emb, prompt_emb, inv_scale)
    probs = jnp.exp(scores - row_lse[None, :]) + jnp.exp(scores - col_lse[:, None])
    grads = ((probs - 2.0 * marks) / (2.0 * pairs)).astype(jnp.bfloat16)
    grads = lax.optimization_barrier(grads)

    prompt_sum = in_two(jnp.dot(grads, prompts, preferred_element_type=jnp.float32) * inv_scale)
    refusal_grad = in_two(
        jnp.dot(grads, prompt_emb, preferred_element_type=jnp.float32) * inv_scale
    )

    def product(start, count):
        right = lax.dynamic_slice_in_dim(refusals, start, count, 1)
        left = [lax.dynamic_slice_in_dim(x, start, count, 1) for x in prompt_sum]
        return (
            dot_first(left[0], refusal_emb)
            + dot_first(right, refusal_grad[0])
            + (dot_first(left[1], refusal_emb) + dot_first(right, refusal_grad[1]))
        )

    came = from_twin(product(given, half), "core")
    kept = (product(own, half) + came).astype(jnp.bfloat16)
    parts = lax.axis_size("x_lo")
    pieces = kept.reshape(parts, half // parts, cuts, width // cuts).transpose(0, 2, 1, 3)
    pieces = pieces.reshape(parts * cuts, half // parts, width // cuts)
    in_layer = jnp.sum(exchange(pieces, SPREAD).astype(jnp.float32), axis=0)
    slices = in_layer.reshape(lax.axis_size(LAYERS), -1, width // cuts)
    done = jnp.sum(exchange(slices, LAYERS), axis=0)
    block = from_all(done, LAYERS).reshape(in_layer.shape)
    return from_all(block, ("core", "x_lo")).reshape(depth, width // cuts)


def solution(mesh):
    split = Mesh(
        mesh.devices.reshape(2, 4, 4, 2, 4, 2), ("x_lo", "z_hi", "z_lo", "core", "y", "x_hi")
    )
    placed = (P(DP, None), P(DP, None), P(None, CUTS), P(DP))
    return jax.shard_map(
        shards, mesh=split, in_specs=placed, out_specs=P(None, CUTS), check_vma=False
    )
```
